32 devices in a mesh: groups: 2 (over y), tp: 4 (over z), rep: 4 (over x, core).
Axes of the slice: x: 2, y: 2, z: 4, core: 2. Of those that a mesh axis runs over, the one named last changes fastest.
Arguments:
- tokens: bfloat16 [2, 32, 16384], P(None, ('groups', 'tp'), 'rep'), parts along dimension 1, may hold values from -6 to 6
- query_weight: bfloat16 [16384, 16384], P('rep', 'tp'), may hold values from -0.046875 to 0.046875
- key_value_weight: bfloat16 [16384, 2048], P('rep', 'tp'), may hold values from -0.046875 to 0.046875
- adapter_down_weight: bfloat16 [8, 16384, 16], P(('groups', 'tp'), 'rep'), parts along dimension 0, may hold values from -0.046875 to 0.046875
- adapter_up_weight: bfloat16 [8, 16, 16384], P(('groups', 'rep'), None, 'tp'), parts along dimension 0, may hold values from -1.5 to 1.5
- request_tenant: int32 [32, 1], P('groups'), parts along dimension 0, may hold values from 0 to 3; in each aligned block of 16 rows (0 to 15, 16 to 31, ...) at most 12 rows name the same one
- tenant_adapter_slot: int32 [4], replicated, may hold values from 0 to 3, each once
- key_value_cache: bfloat16 [32, 192, 2048], P(('groups', 'tp', 'rep')), parts along dimension 0, may hold values from -110 to 110
- cache_length_per_row: int32 [32], P(('groups', 'tp', 'rep')), parts along dimension 0, may hold values from 1 to 192, 1536 in all
Outputs:
- attended: bfloat16 [2, 32, 16384], P(None, ('groups', 'tp', 'rep')), parts along dimension 1
The draws below stay inside these ranges and needn't reach their ends.
There are 2 independent parts, one for each index of `groups`. The reference program is written for one: setup_inputs(seed, part) draws one part's arguments, and reference() takes and returns one part's arrays. A program takes and returns all parts, laid end to end along the dimension named above; an argument that names none is the same for every part. Nothing has to cross between parts.
Inputs may be any that keep to these rules, and one draw needn't show every extreme that they name: `request_tenant`: every tenant has a request; the busiest tenant has exactly 12 requests. `tenant_adapter_slot`: each slot holds the adapters of exactly one tenant. `cache_length_per_row`: some request has exactly 192 cached positions.
All inputs are finite; a program needn't handle non-finite values. No bound on the sum of `cache_length_per_row` on one device may be relied on, other than what follows from the above.
Results may differ from the reference program's by a relative error of at most 0.012.
The reference program's roundings to bfloat16 on the way count: a program that leaves them out, or rounds other values in their place, can miss the bound.
Values may be sent and summed in bfloat16 or wider, within the bound.
A program may use at most 128 MiB of HBM per device.

```python
import math
import jax
import jax.numpy as jnp
import numpy as np

MODEL_WIDTH = 16384
QUERY_HEADS = 128
KEY_VALUE_HEADS = 8
HEAD_SIZE = 128
ADAPTER_RANK = 16
STEPS = 2
CACHE_POSITIONS = 192
REQUEST_TOTAL = 16
TENANT_COUNT = 4
CAP = 12
QUERY_FEATURES = 16384
KVD = 2048


def draw_key_value_cache(key, part):
    key = jax.random.fold_in(key, 11)
    first = jax.random.fold_in(key, 0)
    target_shape = (REQUEST_TOTAL, CACHE_POSITIONS, 2 * KEY_VALUE_HEADS * HEAD_SIZE)
    return jnp.clip(jax.random.normal(first, target_shape, jnp.float32), -6.0, 6.0).astype(jnp.bfloat16)


def shard_levels(stream_key, shape, cuts, least, top_value):
    gain, own = 1.0, jax.random.fold_in(stream_key, 6)
    for position, blocks in cuts:
        draws = jnp.exp(jax.random.uniform(jax.random.fold_in(own, position), (blocks,), jnp.float32, least / len(cuts), top_value / len(cuts)))
        gain = gain * jnp.repeat(draws, shape[position] // blocks).reshape([-1 if axis == position else 1 for axis in range(len(shape))])
    return gain


def profile(count, total, reach, slope):
    portions = [(1 << 20) // math.isqrt(rank ** slope) + 1 for rank in range(2, count + 1)]
    surplus, counts = total - reach - (count - 1), [1] * (count - 1)
    while surplus > 0:
        movable = [i for i in range(count - 1) if counts[i] < reach]
        whole, budget = sum([portions[i] for i in movable]), surplus
        for i in movable:
            addition = min(reach - counts[i], max(1, budget * portions[i] // whole), surplus)
            counts[i] = counts[i] + addition
            surplus = surplus - addition
    return np.array([reach] + counts)


def uneven_parts(key, amount, total, bound, skew):
    if amount == 2:
        one = jax.random.randint(key, (), max(1, total - bound), min(bound, total - 1) + 1)
        return jnp.stack([one, total - one])
    tallies = jnp.asarray(profile(amount, total, bound, skew), jnp.int32)
    twos = (amount - 1) // 2
    source_of, receiver = tallies[1:1 + 2 * twos:2], tallies[2:2 + 2 * twos:2]
    margin = jnp.minimum(source_of - 1, bound - receiver)
    moved = jax.random.randint(jax.random.fold_in(key, 1), (twos,), 0, 1 << 20) % (margin + 1)
    tallies = tallies.at[1:1 + 2 * twos:2].set(source_of - moved).at[2:2 + 2 * twos:2].set(receiver + moved)
    return tallies[jax.random.permutation(jax.random.fold_in(key, 2), amount)]


def routed_block(stream_key, own, number, rows, amount, top, limit, lean):
    ranking = jax.random.permutation(stream_key, amount)
    packed, ordinary = load_shares(amount, rows * top, limit, lean, True), load_shares(amount, rows * top, limit, lean, False)
    places = jnp.arange(amount)

    def named(sizes, offset_by):
        used = int((sizes > 0).sum())
        fixed = max(1, used // 4)
        passed = fixed + (places - fixed + offset_by * (used - fixed)) % max(1, amount - fixed)
        return jnp.zeros((amount,), jnp.int32).at[ranking[jnp.where(places < fixed, places, passed)]].set(jnp.asarray(sizes, jnp.int32))

    sizes = jnp.where(number % 4 == 0, named(packed, number // 4), named(ordinary, number - number // 4 - 1))
    mixed = jax.random.permutation(jax.random.fold_in(own, 3), amount)
    donor, sink = mixed[0:amount // 2 * 2:2], mixed[1:amount // 2 * 2:2]
    room = jnp.minimum(sizes[donor] - 1, limit - sizes[sink]) // 2
    room = jnp.where((donor == ranking[0]) | (sink == ranking[0]) | (sizes[sink] == 0), 0, jnp.maximum(room, 0))
    passed = jax.random.randint(jax.random.fold_in(own, 4), (amount // 2,), 0, 1 << 20) % (room + 1)
    sizes = sizes.at[donor].add(-passed).at[sink].add(passed)
    items = jnp.searchsorted(jnp.cumsum(sizes), jnp.arange(rows * top), side="right").astype(jnp.int32)
    listing = items.reshape(top, rows).T
    listing = listing[jax.random.permutation(jax.random.fold_in(own, 1), rows)]
    offset_by = jax.random.randint(jax.random.fold_in(own, 2), (rows, 1), 0, top)
    return jnp.take_along_axis(listing, (jnp.arange(top)[None, :] + offset_by) % top, axis=1)


def load_shares(count, total, reach, slope, full):
    portions = [(1 << 20) // math.isqrt(rank ** slope) + 1 for rank in range(1, count + 1)]
    largest = reach if full else min(reach, max(-(-total // count), total * portions[0] // sum(portions)))
    least = 1 if total - largest >= count - 1 else 0
    holding, rest = [largest] + [least] * (count - 1), total - largest - least * (count - 1)
    while rest > 0:
        free = [i for i in range(1, count) if holding[i] < largest] or [i for i in range(1, count) if holding[i] < reach]
        whole, left = sum([portions[i] for i in free]), rest
        for i in free:
            extra = min(reach - holding[i], max(1, left * portions[i] // whole), rest)
            holding[i] = holding[i] + extra
            rest = rest - extra
    return np.array(holding)


def noise(own_key, extent, spread, reach, cuts=(), kind=jnp.bfloat16):
    factor_of = shard_levels(own_key, extent, cuts, -0.22, 0.18) if cuts else 1.0
    array = jax.random.normal(own_key, extent, jnp.float32) * spread * factor_of
    return jnp.minimum(jnp.maximum(array, -reach), reach).astype(kind)


def setup_inputs(seed: int = 0, part: int = 0) -> dict:
    streams_of = jax.random.split(jax.random.key(seed), 10)
    own_keys = jax.random.split(jax.random.fold_in(streams_of[9], part), 10)
    tokens = noise(own_keys[0], (STEPS, REQUEST_TOTAL, MODEL_WIDTH), 1.0, 6.0, ((1, 4), (2, 4)))
    query_weight = noise(streams_of[1], (MODEL_WIDTH, QUERY_FEATURES), MODEL_WIDTH ** -0.5, 0.046875, ((0, 4), (1, 4)))
    key_value_weight = noise(streams_of[2], (MODEL_WIDTH, KVD), MODEL_WIDTH ** -0.5, 0.046875, ((0, 4), (1, 4)))
    adapter_down_weight = noise(own_keys[3], (TENANT_COUNT, MODEL_WIDTH, ADAPTER_RANK), MODEL_WIDTH ** -0.5, 0.046875, ((0, 4), (1, 4)))
    adapter_up_weight = noise(own_keys[4], (TENANT_COUNT, ADAPTER_RANK, QUERY_FEATURES), ADAPTER_RANK ** -0.5, 1.5, ((0, 4), (2, 4)))
    request_tenant_keys = jax.random.split(jax.random.fold_in(own_keys[5], 1), REQUEST_TOTAL // REQUEST_TOTAL)
    request_tenant_turns = jax.random.permutation(jax.random.fold_in(own_keys[5], 3), REQUEST_TOTAL // REQUEST_TOTAL)
    request_tenant = jax.vmap(lambda own, number: routed_block(jax.random.fold_in(own_keys[5], 2), own, number, REQUEST_TOTAL, TENANT_COUNT, 1, CAP, 2))(request_tenant_keys, request_tenant_turns).reshape((REQUEST_TOTAL, 1))
    tenant_adapter_slot = jax.random.permutation(streams_of[6], TENANT_COUNT).astype(jnp.int32)
    key_value_cache = draw_key_value_cache(jax.random.fold_in(jax.random.fold_in(streams_of[9], part), 71), part)
    cache_length_per_row = uneven_parts(own_keys[8], REQUEST_TOTAL, REQUEST_TOTAL * CACHE_POSITIONS // 2, CACHE_POSITIONS, 2).astype(jnp.int32)
    return {"tokens": tokens, "query_weight": query_weight, "key_value_weight": key_value_weight, "adapter_down_weight": adapter_down_weight, "adapter_up_weight": adapter_up_weight, "request_tenant": request_tenant, "tenant_adapter_slot": tenant_adapter_slot, "key_value_cache": key_value_cache, "cache_length_per_row": cache_length_per_row}


def reference(tokens, query_weight, key_value_weight, adapter_down_weight, adapter_up_weight, request_tenant, tenant_adapter_slot, key_value_cache, cache_length_per_row):
    labels = jnp.arange(TENANT_COUNT, dtype=jnp.int32)
    slot_row = jnp.sum(jnp.where(request_tenant == labels[None, :], tenant_adapter_slot[None, :], 0), axis=1).astype(jnp.int32)
    onehot = slot_row[:, None] == labels[None, :]
    flattened_down_weight = jnp.transpose(adapter_down_weight, (1, 0, 2)).reshape(MODEL_WIDTH, TENANT_COUNT * ADAPTER_RANK)
    flattened_up_weight = adapter_up_weight.reshape(TENANT_COUNT * ADAPTER_RANK, QUERY_FEATURES)
    half_width = KEY_VALUE_HEADS * HEAD_SIZE
    query_group = QUERY_HEADS // KEY_VALUE_HEADS
    stored_keys = key_value_cache[:, :, :half_width].reshape(REQUEST_TOTAL, CACHE_POSITIONS, KEY_VALUE_HEADS, HEAD_SIZE).astype(jnp.float32)
    stored_values = key_value_cache[:, :, half_width:].reshape(REQUEST_TOTAL, CACHE_POSITIONS, KEY_VALUE_HEADS, HEAD_SIZE).astype(jnp.float32)
    incoming_keys = []
    incoming_values = []
    results = []
    for step in range(STEPS):
        hidden = tokens[step]
        base = jnp.dot(hidden, query_weight, preferred_element_type=jnp.float32)
        key_value_rows = jnp.dot(hidden, key_value_weight, preferred_element_type=jnp.float32).astype(jnp.bfloat16)
        lowrank_all = jnp.dot(hidden, flattened_down_weight, preferred_element_type=jnp.float32).reshape(REQUEST_TOTAL, TENANT_COUNT, ADAPTER_RANK)
        lowrank = jnp.where(onehot[:, :, None], lowrank_all, 0.0).astype(jnp.bfloat16)
        delta = jnp.dot(lowrank.reshape(REQUEST_TOTAL, TENANT_COUNT * ADAPTER_RANK), flattened_up_weight, preferred_element_type=jnp.float32)
        query_vector = (base + delta).astype(jnp.bfloat16)
        incoming_keys.append(key_value_rows[:, :half_width].reshape(REQUEST_TOTAL, 1, KEY_VALUE_HEADS, HEAD_SIZE).astype(jnp.float32))
        incoming_values.append(key_value_rows[:, half_width:].reshape(REQUEST_TOTAL, 1, KEY_VALUE_HEADS, HEAD_SIZE).astype(jnp.float32))
        keys = jnp.concatenate([stored_keys] + incoming_keys, axis=1)
        vals = jnp.concatenate([stored_values] + incoming_values, axis=1)
        head_outputs = query_vector.reshape(REQUEST_TOTAL, KEY_VALUE_HEADS, query_group, HEAD_SIZE).astype(jnp.float32)
        scores = jnp.einsum("bgmd,bjgd->bgmj", head_outputs, keys) * (HEAD_SIZE ** -0.5)
        spots = jnp.arange(CACHE_POSITIONS + step + 1, dtype=jnp.int32)
        valid = (spots[None, :] < cache_length_per_row[:, None]) | (spots[None, :] >= CACHE_POSITIONS)
        scores = jnp.where(valid[:, None, None, :], scores, -jnp.inf)
        top = jnp.max(scores, axis=-1, keepdims=True)
        weights = jnp.exp(scores - top)
        probs = (weights / jnp.sum(weights, axis=-1, keepdims=True)).astype(jnp.bfloat16)
        out = jnp.einsum("bgmj,bjgd->bgmd", probs.astype(jnp.float32), vals)
        results.append(out.astype(jnp.bfloat16).reshape(REQUEST_TOTAL, QUERY_FEATURES))
    return jnp.stack(results)
```

```python
import functools

import jax
import jax.numpy as jnp
from jax import lax
from jax.experimental import pallas as pl
from jax.experimental.pallas import tpu as pltpu
from jax.sharding import PartitionSpec as P

KEY_VALUE_HEADS = 8
HEAD_SIZE = 128
CHUNK = 512
DEFER = 2
MESH = pl.DeviceIdType.MESH


def peer(tp, rep):
    return {"tp": tp, "rep": rep}


def remote(src, dst, send_sem, recv_sem, tp, rep):
    return pltpu.make_async_remote_copy(
        src_ref=src,
        dst_ref=dst,
        send_sem=send_sem,
        recv_sem=recv_sem,
        device_id=peer(tp, rep),
        device_id_type=MESH,
    )


def fused_kernel(
    tp_count,
    rep_count,
    tokens,
    query_weight,
    key_value_weight,
    adapter_down_weight,
    adapter_up_weight,
    request_tenant,
    tenant_adapter_slot,
    key_value_cache,
    cache_length,
    out,
    own_tokens,
    own_wide,
    gathered,
    hidden,
    weights,
    down,
    up,
    cache,
    low_send,
    low_recv,
    low_masked,
    held,
    part_send,
    part_recv,
    stage,
    query_send,
    query_recv,
    kv_send,
    kv_recv,
    weight_sem,
    load_sem,
    gather_send_sem,
    gather_recv_sem,
    low_send_sem,
    low_recv_sem,
    part_send_sem,
    part_recv_sem,
    query_send_sem,
    query_recv_sem,
    kv_send_sem,
    kv_recv_sem,
):
    t = lax.axis_index("tp")
    r = lax.axis_index("rep")
    steps, rows_rep, depth = tokens.shape
    half_depth = depth // 2
    group_rows = steps * tp_count
    rows = group_rows * rep_count
    query_columns = query_weight.shape[1]
    query_chunks = query_columns // CHUNK
    chunk_heads = CHUNK // HEAD_SIZE
    rank = adapter_down_weight.shape[2]
    positions = key_value_cache.shape[1]
    half_width = KEY_VALUE_HEADS * HEAD_SIZE

    barrier = pltpu.get_barrier_semaphore()
    for dt in range(tp_count):
        for dr in range(rep_count):
            if dt or dr:
                pl.semaphore_signal(
                    barrier,
                    inc=1,
                    device_id=peer(lax.rem(t + dt, tp_count), lax.rem(r + dr, rep_count)),
                    device_id_type=MESH,
                )

    load_tokens = pltpu.make_async_copy(tokens, own_tokens, load_sem.at[0])
    load_down = pltpu.make_async_copy(adapter_down_weight.at[0], down, load_sem.at[1])
    load_up = pltpu.make_async_copy(adapter_up_weight.at[0], up, load_sem.at[2])
    load_cache = pltpu.make_async_copy(key_value_cache.at[0], cache, load_sem.at[3])
    load_tokens.start()
    load_down.start()
    load_weights = [
        pltpu.make_async_copy(key_value_weight, weights.at[0], weight_sem.at[0])
    ] + [
        pltpu.make_async_copy(
            query_weight.at[:, pl.ds(c * CHUNK, CHUNK)], weights.at[c + 1], weight_sem.at[c + 1]
        )
        for c in range(query_chunks)
    ]
    load_weights[0].start()
    load_up.start()
    for copy in load_weights[1:]:
        copy.start()
    load_cache.start()

    load_tokens.wait()
    for s in range(steps):
        wide = own_tokens[s].astype(jnp.float32)
        for h in range(2):
            first = h * steps * rows_rep + s * rows_rep
            own_wide[first : first + rows_rep, :] = wide[:, h * half_depth : (h + 1) * half_depth]
    gathered[t] = own_wide[...].astype(jnp.bfloat16)
    pl.semaphore_wait(barrier, tp_count * rep_count - 1)

    sends = []
    gathers = []
    for d in range(tp_count - 1, 0, -1):
        to = lax.rem(t + d, tp_count)
        copy = remote(
            gathered.at[t], gathered.at[t], gather_send_sem.at[to], gather_recv_sem.at[t], to, r
        )
        copy.start()
        sends.append(copy)
        gathers.append(
            remote(
                gathered.at[to], gathered.at[to], gather_send_sem.at[to], gather_recv_sem.at[to], to, r
            )
        )

    row = lax.broadcasted_iota(jnp.int32, (rows, HEAD_SIZE), 0)
    request = lax.rem(row // steps, tp_count) * rep_count + row // group_rows
    tenant = jnp.zeros_like(row)
    for i in range(tp_count * rep_count):
        tenant = jnp.where(request == i, request_tenant[i, 0], tenant)
    slot = jnp.zeros_like(row)
    for label in range(tenant_adapter_slot.shape[0]):
        slot = jnp.where(tenant == label, tenant_adapter_slot[label], slot)
    matched = slot == r

    picked = lax.broadcasted_iota(jnp.int32, (rows, 2 * rows), 0)
    place = lax.broadcasted_iota(jnp.int32, (rows, 2 * rows), 1)
    source = (
        lax.rem(picked // steps, tp_count) * (2 * steps * rows_rep)
        + lax.rem(picked, steps) * rows_rep
        + picked // group_rows
    )

    for copy in gathers:
        copy.wait_recv()
    everything = gathered[...].reshape(2 * rows, half_depth)
    for h in range(2):
        order = jnp.where(place == source + h * steps * rows_rep, 1.0, 0.0).astype(jnp.bfloat16)
        hidden[:, h * half_depth : (h + 1) * half_depth] = jnp.dot(
            order, everything, preferred_element_type=jnp.float32
        ).astype(jnp.bfloat16)

    load_down.wait()
    low_send[...] = jnp.zeros_like(low_send)
    low_send[:, 0:rank] = jnp.dot(hidden[...], down[...], preferred_element_type=jnp.float32)
    low_copies = []
    for d in range(tp_count):
        to = lax.rem(t + d, tp_count)
        source_rep = lax.rem(t + d, rep_count)
        copy = remote(low_send, low_recv.at[r], low_send_sem.at[d], low_recv_sem.at[r], to, t)
        arrival = remote(
            low_send,
            low_recv.at[source_rep],
            low_send_sem.at[d],
            low_recv_sem.at[source_rep],
            to,
            t,
        )
        low_copies.append((copy, arrival))
        if d == 0:
            pl.when(r != t)(copy.start)
        else:
            copy.start()

    @pl.when(r == t)
    def _():
        low_recv[r] = low_send[...]

    def multiply(c):
        load_weights[c].wait()
        return jnp.dot(hidden[...], weights[c], preferred_element_type=jnp.float32)

    def send_parts(c, value):
        part_send[c] = value.reshape(rep_count, group_rows, CHUNK)
        for d in range(1, rep_count):
            to = lax.rem(r + d, rep_count)
            copy = remote(
                part_send.at[c, to],
                part_recv.at[c, r],
                part_send_sem.at[c, to],
                part_recv_sem.at[c, r],
                t,
                to,
            )
            copy.start()
            sends.append(copy)

    def total(c):
        value = part_send[c, r]
        for d in range(1, rep_count):
            place = lax.rem(r + d, rep_count)
            remote(
                part_send.at[c, place],
                part_recv.at[c, place],
                part_send_sem.at[c, place],
                part_recv_sem.at[c, place],
                t,
                place,
            ).wait_recv()
            value = value + part_recv[c, place]
        return value

    arrivals = {}

    def send_rows(name, source_buffer, place_of, send_sem, recv_sem):
        arrivals[name] = []
        for d in range(tp_count - 1, 0, -1):
            to = lax.rem(t + d, tp_count)
            copy = remote(
                source_buffer.at[to], place_of(t), send_sem.at[to], recv_sem.at[t], to, r
            )
            copy.start()
            sends.append(copy)
            arrivals[name].append(
                remote(source_buffer.at[to], place_of(to), send_sem.at[to], recv_sem.at[to], to, r)
            )

    def finish_key_value():
        value = total(0)
        for place in range(tp_count):
            for s in range(steps):
                for h in range(chunk_heads):
                    at = s * chunk_heads + h
                    kv_send[place, at : at + 1, :] = value[
                        place * steps + s : place * steps + s + 1,
                        h * HEAD_SIZE : (h + 1) * HEAD_SIZE,
                    ]
        send_rows("kv", kv_send, lambda i: kv_recv.at[i], kv_send_sem, kv_recv_sem)
        kv_recv[t] = kv_send[t]

    per_group = query_columns // HEAD_SIZE // 2 // chunk_heads

    def finish_query(c):
        value = total(c + 1)
        half, inside = c // per_group, c % per_group
        for h in range(chunk_heads):
            stage[half, :, inside * chunk_heads + h, :] = value[
                :, h * HEAD_SIZE : (h + 1) * HEAD_SIZE
            ]
        if inside == per_group - 1:
            query_send[half] = (
                stage[half].astype(jnp.bfloat16).reshape(tp_count, steps, -1, HEAD_SIZE)
            )
            send_rows(
                half,
                query_send.at[half],
                lambda i: query_recv.at[half, i],
                query_send_sem.at[half],
                query_recv_sem.at[half],
            )
            query_recv[half, t] = query_send[half, t]

    def adapted(c, value):
        return value + jnp.dot(
            low_masked[...],
            up[:, c * CHUNK : (c + 1) * CHUNK],
            preferred_element_type=jnp.float32,
        )

    heads_of = per_group * chunk_heads

    def attend_half(half):
        if half == 0:
            load_cache.wait()
            for copy in arrivals["kv"]:
                copy.wait_recv()
        for copy in arrivals[half]:
            copy.wait_recv()
        length = cache_length[0]
        scale = HEAD_SIZE**-0.5
        valid = lax.broadcasted_iota(jnp.int32, (steps * heads_of, positions), 1) < length
        extra = steps * chunk_heads
        column = lax.broadcasted_iota(jnp.int32, (steps * heads_of, extra), 1)
        step_of = lax.broadcasted_iota(jnp.int32, (steps * heads_of, extra), 0) // heads_of
        causal = column // chunk_heads <= step_of
        for tt in range(tp_count):
            g = 2 * tt + half
            query = query_recv[half, tt].reshape(steps * heads_of, HEAD_SIZE)
            keys = cache[:, g * HEAD_SIZE : (g + 1) * HEAD_SIZE]
            values = cache[:, half_width + g * HEAD_SIZE : half_width + (g + 1) * HEAD_SIZE]
            holder, inner = g // chunk_heads, g % chunk_heads
            new_keys = kv_recv[holder].astype(jnp.bfloat16)
            new_values = kv_recv[tp_count // 2 + holder].astype(jnp.bfloat16).astype(jnp.float32)
            contract = (((1,), (1,)), ((), ()))
            older = (
                lax.dot_general(query, keys, contract, preferred_element_type=jnp.float32) * scale
            )
            newer = (
                lax.dot_general(query, new_keys, contract, preferred_element_type=jnp.float32)
                * scale
            )
            older = jnp.where(valid, older, -jnp.inf)
            newer = jnp.where(
                causal & (lax.rem(column, chunk_heads) == inner), newer, -jnp.inf
            )
            top = jnp.maximum(
                jnp.max(older, axis=1, keepdims=True), jnp.max(newer, axis=1, keepdims=True)
            )
            older = jnp.exp(older - top)
            newer = jnp.exp(newer - top)
            whole = jnp.sum(older, axis=1, keepdims=True) + jnp.sum(newer, axis=1, keepdims=True)
            older = (older / whole).astype(jnp.bfloat16)
            newer = (newer / whole).astype(jnp.bfloat16).astype(jnp.float32)
            mixed = jnp.dot(older, values, preferred_element_type=jnp.float32)
            for s in range(steps):
                at = s * chunk_heads + inner
                mixed = mixed + newer[:, at : at + 1] * new_values[at : at + 1, :]
            mixed = mixed.astype(jnp.bfloat16)
            for s in range(steps):
                out[s, g * heads_of : (g + 1) * heads_of, :] = mixed[
                    s * heads_of : (s + 1) * heads_of, :
                ]

    send_parts(0, multiply(0))
    for c in range(DEFER):
        held[c] = multiply(c + 1)
    for d, (_, arrival) in enumerate(low_copies):
        if d == 0:
            pl.when(r != t)(arrival.wait_recv)
        else:
            arrival.wait_recv()
    low_total = low_recv[0]
    for i in range(1, rep_count):
        low_total = low_total + low_recv[i]
    low_masked[...] = jnp.where(matched, low_total, 0.0).astype(jnp.bfloat16)[:, 0:rank]
    load_up.wait()
    for c in range(DEFER):
        send_parts(c + 1, adapted(c, held[c]))
    finish_key_value()
    for c in range(DEFER, query_chunks):
        send_parts(c + 1, adapted(c, multiply(c + 1)))
        finish_query(c - DEFER)
    attended = per_group <= query_chunks - DEFER
    if attended:
        attend_half(0)
    for c in range(query_chunks - DEFER, query_chunks):
        finish_query(c)
    if not attended:
        attend_half(0)
    attend_half(1)

    for copy in sends:
        copy.wait_send()
    for d, (copy, _) in enumerate(low_copies):
        if d == 0:
            pl.when(r != t)(copy.wait_send)
        else:
            copy.wait_send()


def fused(*operands):
    tokens, query_weight, key_value_weight, down, up, request_tenant, slots, cache, lengths = operands
    tp_count = lax.axis_size("tp")
    rep_count = lax.axis_size("rep")
    steps, rows_rep, depth = tokens.shape
    columns = query_weight.shape[1]
    chunks = columns // CHUNK + 1
    group_rows = steps * tp_count
    rows = group_rows * rep_count
    heads_of = columns // HEAD_SIZE // 2
    bf16, f32 = jnp.bfloat16, jnp.float32
    dma = pltpu.SemaphoreType.DMA
    anywhere = pl.BlockSpec(memory_space=pl.ANY)
    scalars = pl.BlockSpec(memory_space=pltpu.SMEM)
    heads = tp_count * columns // HEAD_SIZE
    result = pl.pallas_call(
        functools.partial(fused_kernel, tp_count, rep_count),
        out_shape=jax.ShapeDtypeStruct((steps, heads, HEAD_SIZE), bf16),
        in_specs=[anywhere] * 5 + [scalars] * 2 + [anywhere, scalars],
        out_specs=pl.BlockSpec(memory_space=pltpu.VMEM),
        scratch_shapes=[
            pltpu.VMEM(tokens.shape, bf16),
            pltpu.VMEM((2 * steps * rows_rep, depth // 2), f32),
            pltpu.VMEM((tp_count, 2 * steps * rows_rep, depth // 2), bf16),
            pltpu.VMEM((rows, depth), bf16),
            pltpu.VMEM((chunks, depth, CHUNK), bf16),
            pltpu.VMEM(down.shape[1:], bf16),
            pltpu.VMEM(up.shape[1:], bf16),
            pltpu.VMEM(cache.shape[1:], bf16),
            pltpu.VMEM((rows, HEAD_SIZE), f32),
            pltpu.VMEM((rep_count, rows, HEAD_SIZE), f32),
            pltpu.VMEM((rows, down.shape[2]), bf16),
            pltpu.VMEM((DEFER, rows, CHUNK), f32),
            pltpu.VMEM((chunks, rep_count, group_rows, CHUNK), f32),
            pltpu.VMEM((chunks, rep_count, group_rows, CHUNK), f32),
            pltpu.VMEM((2, group_rows, heads_of, HEAD_SIZE), f32),
            pltpu.VMEM((2, tp_count, steps, heads_of, HEAD_SIZE), bf16),
            pltpu.VMEM((2, tp_count, steps, heads_of, HEAD_SIZE), bf16),
            pltpu.VMEM((tp_count, steps * CHUNK // HEAD_SIZE, HEAD_SIZE), f32),
            pltpu.VMEM((tp_count, steps * CHUNK // HEAD_SIZE, HEAD_SIZE), f32),
            dma((chunks,)),
            dma((4,)),
            dma((tp_count,)),
            dma((tp_count,)),
            dma((tp_count,)),
            dma((rep_count,)),
            dma((chunks, rep_count)),
            dma((chunks, rep_count)),
            dma((2, tp_count)),
            dma((2, tp_count)),
            dma((tp_count,)),
            dma((tp_count,)),
        ],
        compiler_params=pltpu.CompilerParams(
            collective_id=0, has_side_effects=True, vmem_limit_bytes=60 * 1024 * 1024
        ),
    )(*operands)
    return result.reshape(steps, 1, heads * HEAD_SIZE)


def fits(tokens, query_weight, key_value_weight, down, up, request_tenant, slots, cache, lengths):
    tp_count = lax.axis_size("tp")
    rep_count = lax.axis_size("rep")
    columns = query_weight.shape[1]
    return (
        tp_count == rep_count
        and tp_count % 2 == 0
        and tokens.shape[0] == 2
        and tokens.shape[0] * tp_count == 8
        and tokens.shape[1] == rep_count
        and down.shape[0] == 1
        and up.shape[0] == 1
        and cache.shape[0] == 1
        and key_value_weight.shape[1] == CHUNK
        and columns == 2 * 16 * HEAD_SIZE
        and tokens.shape[2] <= 4096
    )


def slot_lookup(request_tenant, tenant_adapter_slot):
    labels = jnp.arange(tenant_adapter_slot.shape[0], dtype=jnp.int32)
    return jnp.sum(
        jnp.where(request_tenant == labels[None, :], tenant_adapter_slot[None, :], 0), axis=1
    )


def attend(query_matrix, incoming_key_value, key_value_cache, cache_length_per_row):
    row_indices = query_matrix.shape[0]
    position_span = key_value_cache.shape[1]
    incoming_token = incoming_key_value.shape[0]
    half_width = KEY_VALUE_HEADS * HEAD_SIZE
    head_outputs = query_matrix.reshape(row_indices, KEY_VALUE_HEADS, -1, HEAD_SIZE)
    stored_keys = key_value_cache[:, :, :half_width].reshape(
        row_indices, position_span, KEY_VALUE_HEADS, HEAD_SIZE
    )
    stored_values = key_value_cache[:, :, half_width:].reshape(
        row_indices, position_span, KEY_VALUE_HEADS, HEAD_SIZE
    )
    incoming_keys = jnp.transpose(incoming_key_value[:, :, :half_width], (1, 0, 2)).reshape(
        row_indices, incoming_token, KEY_VALUE_HEADS, HEAD_SIZE
    )
    incoming_values = jnp.transpose(incoming_key_value[:, :, half_width:], (1, 0, 2)).reshape(
        row_indices, incoming_token, KEY_VALUE_HEADS, HEAD_SIZE
    )
    scale = HEAD_SIZE ** (-0.5)
    older = (
        jnp.einsum("bgmd,bjgd->bgmj", head_outputs, stored_keys, preferred_element_type=jnp.float32)
        * scale
    )
    newer = (
        jnp.einsum(
            "bgmd,bjgd->bgmj", head_outputs, incoming_keys, preferred_element_type=jnp.float32
        )
        * scale
    )
    valid = jnp.arange(position_span, dtype=jnp.int32)[None, :] < cache_length_per_row[:, None]
    older = jnp.where(valid[:, None, None, :], older, -jnp.inf)
    top = jnp.maximum(jnp.max(older, axis=-1), jnp.max(newer, axis=-1))[..., None]
    older_exp = jnp.exp(older - top)
    newer_exp = jnp.exp(newer - top)
    total = jnp.sum(older_exp, axis=-1, keepdims=True) + jnp.sum(newer_exp, axis=-1, keepdims=True)
    older_prob = (older_exp / total).astype(jnp.bfloat16)
    newer_prob = (newer_exp / total).astype(jnp.bfloat16)
    mixed = jnp.einsum(
        "bgmj,bjgd->bgmd", older_prob, stored_values, preferred_element_type=jnp.float32
    )
    mixed = mixed + jnp.einsum(
        "bgmj,bjgd->bgmd", newer_prob, incoming_values, preferred_element_type=jnp.float32
    )
    return mixed.astype(jnp.bfloat16).reshape(row_indices, -1)


def shards(
    tokens,
    query_weight,
    key_value_weight,
    adapter_down_weight,
    adapter_up_weight,
    request_tenant,
    tenant_adapter_slot,
    key_value_cache,
    cache_length_per_row,
):
    operands = (
        tokens,
        query_weight,
        key_value_weight,
        adapter_down_weight,
        adapter_up_weight,
        request_tenant,
        tenant_adapter_slot,
        key_value_cache,
        cache_length_per_row,
    )
    if fits(*operands):
        return fused(*operands)
    tp_count = lax.axis_size("tp")
    rep_count = lax.axis_size("rep")
    rep_place = lax.axis_index("rep")
    rows_all = request_tenant.shape[0]
    request_slots = adapter_down_weight.shape[0]
    replicated_slots = adapter_up_weight.shape[0]
    adapter_rank_size = adapter_down_weight.shape[2]
    query_columns = query_weight.shape[1]
    kv_cols = key_value_weight.shape[1]
    local_rows = rows_all // (tp_count * rep_count)
    slot_row = slot_lookup(request_tenant, tenant_adapter_slot)
    flattened_down_weight = jnp.transpose(adapter_down_weight, (1, 0, 2)).reshape(
        adapter_down_weight.shape[1], request_slots * adapter_rank_size
    )
    flattened_up_weight = adapter_up_weight.reshape(
        replicated_slots * adapter_rank_size, query_columns
    )
    rep_labels = rep_place * replicated_slots + jnp.arange(replicated_slots, dtype=jnp.int32)
    rep_match = slot_row[:, None] == rep_labels[None, :]
    steps = tokens.shape[0]
    count = tokens.shape[0]
    piece = lax.all_gather(tokens, "tp", axis=1, tiled=True)
    flat = piece.reshape(-1, piece.shape[2])
    joined = jnp.concatenate(
        [
            jnp.dot(flat, query_weight, preferred_element_type=jnp.float32),
            jnp.dot(flat, key_value_weight, preferred_element_type=jnp.float32),
            jnp.dot(flat, flattened_down_weight, preferred_element_type=jnp.float32),
        ],
        axis=1,
    )
    terms = joined.reshape(piece.shape[0], piece.shape[1], -1)
    q_part = terms[:, :, :query_columns]
    kv_part = terms[:, :, query_columns : query_columns + kv_cols]
    low_part = terms[:, :, query_columns + kv_cols :]
    low_sum = lax.psum(low_part, "rep")
    low_all = lax.all_gather(low_sum.astype(jnp.bfloat16), "tp", axis=2, tiled=True)
    low_rep = lax.dynamic_slice_in_dim(
        low_all,
        rep_place * replicated_slots * adapter_rank_size,
        replicated_slots * adapter_rank_size,
        2,
    )
    low_rep = low_rep.reshape(count, rows_all, replicated_slots, adapter_rank_size)
    masked = jnp.where(rep_match[None, :, :, None], low_rep, jnp.zeros((), jnp.bfloat16))
    delta = jnp.dot(
        masked.reshape(count * rows_all, replicated_slots * adapter_rank_size),
        flattened_up_weight,
        preferred_element_type=jnp.float32,
    )
    q_part = (q_part + delta.reshape(count, rows_all, query_columns)).reshape(
        count, tp_count, rep_count * local_rows, query_columns
    )
    kv_part = kv_part.reshape(count, tp_count, rep_count * local_rows, kv_cols)
    q_sum = lax.psum_scatter(q_part, "rep", scatter_dimension=2, tiled=True)
    kv_sum = lax.psum_scatter(kv_part, "rep", scatter_dimension=2, tiled=True)
    query_vector = lax.all_to_all(
        q_sum.astype(jnp.bfloat16), "tp", split_axis=1, concat_axis=3, tiled=True
    )
    key_value_rows = lax.all_to_all(
        kv_sum.astype(jnp.bfloat16), "tp", split_axis=1, concat_axis=3, tiled=True
    )
    query_vector, key_value_rows = (
        query_vector.reshape(count, local_rows, -1),
        key_value_rows.reshape(count, local_rows, -1),
    )
    results = []
    for step in range(steps):
        results.append(
            attend(
                query_vector[step],
                key_value_rows[: step + 1],
                key_value_cache,
                cache_length_per_row,
            )
        )
    return jnp.stack(results)


def solution(mesh):
    placed = (
        P(None, ("groups", "tp"), "rep"),
        P("rep", "tp"),
        P("rep", "tp"),
        P(("groups", "tp"), "rep", None),
        P(("groups", "rep"), None, "tp"),
        P("groups", None),
        P(),
        P(("groups", "tp", "rep"), None, None),
        P(("groups", "tp", "rep")),
    )
    return jax.shard_map(
        shards,
        mesh=mesh,
        in_specs=placed,
        out_specs=P(None, ("groups", "tp", "rep"), None),
        check_vma=False,
    )
```

```python
import functools

import jax
import jax.numpy as jnp
from jax import lax
from jax.experimental import pallas as pl
from jax.experimental.pallas import tpu as pltpu
from jax.sharding import PartitionSpec as P

KEY_VALUE_HEADS = 8
HEAD_SIZE = 128
CHUNK = 512
DEFER = 2
BEFORE = 2
AHEAD = 3
MESH = pl.DeviceIdType.MESH


def peer(tp, rep):
    return {"tp": tp, "rep": rep}


def remote(src, dst, send_sem, recv_sem, tp, rep):
    return pltpu.make_async_remote_copy(
        src_ref=src,
        dst_ref=dst,
        send_sem=send_sem,
        recv_sem=recv_sem,
        device_id=peer(tp, rep),
        device_id_type=MESH,
    )


def fused_kernel(
    tp_count,
    rep_count,
    tokens,
    query_weight,
    key_value_weight,
    adapter_down_weight,
    adapter_up_weight,
    request_tenant,
    tenant_adapter_slot,
    key_value_cache,
    cache_length,
    out,
    own_tokens,
    own_wide,
    gathered,
    hidden,
    weights,
    down,
    up,
    cache,
    low_send,
    low_recv,
    low_masked,
    held,
    part_send,
    part_recv,
    stage,
    query_send,
    query_recv,
    kv_send,
    kv_recv,
    mix,
    weight_sem,
    load_sem,
    gather_send_sem,
    gather_recv_sem,
    low_send_sem,
    low_recv_sem,
    part_send_sem,
    part_recv_sem,
    query_send_sem,
    query_recv_sem,
    kv_send_sem,
    kv_recv_sem,
):
    t = lax.axis_index("tp")
    r = lax.axis_index("rep")
    steps, rows_rep, depth = tokens.shape
    half_depth = depth // 2
    group_rows = steps * tp_count
    rows = group_rows * rep_count
    query_columns = query_weight.shape[1]
    query_chunks = query_columns // CHUNK
    chunk_heads = CHUNK // HEAD_SIZE
    rank = adapter_down_weight.shape[1]
    positions = key_value_cache.shape[1]
    half_width = KEY_VALUE_HEADS * HEAD_SIZE

    barrier = pltpu.get_barrier_semaphore()
    for dt in range(tp_count):
        for dr in range(rep_count):
            if dt or dr:
                pl.semaphore_signal(
                    barrier,
                    inc=1,
                    device_id=peer(lax.rem(t + dt, tp_count), lax.rem(r + dr, rep_count)),
                    device_id_type=MESH,
                )

    load_tokens = pltpu.make_async_copy(tokens, own_tokens, load_sem.at[0])
    load_down = pltpu.make_async_copy(adapter_down_weight.at[0], down, load_sem.at[1])
    load_up = pltpu.make_async_copy(adapter_up_weight.at[0], up, load_sem.at[2])
    load_cache = pltpu.make_async_copy(key_value_cache.at[0], cache, load_sem.at[3])
    load_tokens.start()
    load_down.start()
    load_weights = [
        pltpu.make_async_copy(key_value_weight, weights.at[0], weight_sem.at[0])
    ] + [
        pltpu.make_async_copy(
            query_weight.at[:, pl.ds(c * CHUNK, CHUNK)], weights.at[c + 1], weight_sem.at[c + 1]
        )
        for c in range(query_chunks)
    ]
    load_up.start()
    started = []

    def start_until(count):
        while len(started) < min(count, query_chunks + 1):
            load_weights[len(started)].start()
            started.append(True)
            if len(started) == query_chunks + 1:
                load_cache.start()

    start_until(BEFORE)

    load_tokens.wait()
    for s in range(steps):
        wide = own_tokens[s].astype(jnp.float32)
        for h in range(2):
            first = h * steps * rows_rep + s * rows_rep
            own_wide[first : first + rows_rep, :] = wide[:, h * half_depth : (h + 1) * half_depth]
    gathered[t] = own_wide[...].astype(jnp.bfloat16)
    pl.semaphore_wait(barrier, tp_count * rep_count - 1)

    sends = []
    gathers = []
    for d in range(tp_count - 1, 0, -1):
        to = lax.rem(t + d, tp_count)
        copy = remote(
            gathered.at[t], gathered.at[t], gather_send_sem.at[to], gather_recv_sem.at[t], to, r
        )
        copy.start()
        sends.append(copy)
        gathers.append(
            remote(
                gathered.at[to], gathered.at[to], gather_send_sem.at[to], gather_recv_sem.at[to], to, r
            )
        )

    start_until(AHEAD)

    row = lax.broadcasted_iota(jnp.int32, (rows, HEAD_SIZE), 0)
    request = lax.rem(row // steps, tp_count) * rep_count + row // group_rows
    tenant = jnp.zeros_like(row)
    for i in range(tp_count * rep_count):
        tenant = jnp.where(request == i, request_tenant[0, i], tenant)
    slot = jnp.zeros_like(row)
    for label in range(tenant_adapter_slot.shape[0]):
        slot = jnp.where(tenant == label, tenant_adapter_slot[label], slot)
    matched = slot == r

    picked = lax.broadcasted_iota(jnp.int32, (rows, 2 * rows), 0)
    place = lax.broadcasted_iota(jnp.int32, (rows, 2 * rows), 1)
    source = (
        lax.rem(picked // steps, tp_count) * (2 * steps * rows_rep)
        + lax.rem(picked, steps) * rows_rep
        + picked // group_rows
    )

    for copy in gathers:
        copy.wait_recv()
    everything = gathered[...].reshape(2 * rows, half_depth)
    for h in range(2):
        order = jnp.where(place == source + h * steps * rows_rep, 1.0, 0.0).astype(jnp.bfloat16)
        hidden[:, h * half_depth : (h + 1) * half_depth] = jnp.dot(
            order, everything, preferred_element_type=jnp.float32
        ).astype(jnp.bfloat16)

    load_down.wait()
    low_send[...] = jnp.zeros_like(low_send)
    low_send[:, 0:rank] = lax.dot_general(
        hidden[...], down[...], (((1,), (1,)), ((), ())), preferred_element_type=jnp.float32
    )
    low_copies = []
    for d in range(tp_count):
        to = lax.rem(t + d, tp_count)
        source_rep = lax.rem(t + d, rep_count)
        copy = remote(low_send, low_recv.at[r], low_send_sem.at[d], low_recv_sem.at[r], to, t)
        arrival = remote(
            low_send,
            low_recv.at[source_rep],
            low_send_sem.at[d],
            low_recv_sem.at[source_rep],
            to,
            t,
        )
        low_copies.append((copy, arrival))
        if d == 0:
            pl.when(r != t)(copy.start)
        else:
            copy.start()

    @pl.when(r == t)
    def _():
        low_recv[r] = low_send[...]

    def multiply(c):
        load_weights[c].wait()
        start_until(c + 1 + AHEAD)
        return jnp.dot(hidden[...], weights[c], preferred_element_type=jnp.float32)

    def send_parts(c, value):
        part_send[c] = value.reshape(rep_count, group_rows, CHUNK)
        for d in range(1, rep_count):
            to = lax.rem(r + d, rep_count)
            copy = remote(
                part_send.at[c, to],
                part_recv.at[c, r],
                part_send_sem.at[c, to],
                part_recv_sem.at[c, r],
                t,
                to,
            )
            copy.start()
            sends.append(copy)

    def total(c):
        value = part_send[c, r]
        for d in range(1, rep_count):
            place = lax.rem(r + d, rep_count)
            remote(
                part_send.at[c, place],
                part_recv.at[c, place],
                part_send_sem.at[c, place],
                part_recv_sem.at[c, place],
                t,
                place,
            ).wait_recv()
            value = value + part_recv[c, place]
        return value

    arrivals = {}

    def send_rows(name, source_buffer, place_of, send_sem, recv_sem):
        arrivals[name] = []
        for d in range(tp_count - 1, 0, -1):
            to = lax.rem(t + d, tp_count)
            copy = remote(
                source_buffer.at[to], place_of(t), send_sem.at[to], recv_sem.at[t], to, r
            )
            copy.start()
            sends.append(copy)
            arrivals[name].append(
                remote(source_buffer.at[to], place_of(to), send_sem.at[to], recv_sem.at[to], to, r)
            )

    def finish_key_value():
        value = total(0)
        for place in range(tp_count):
            for s in range(steps):
                for h in range(chunk_heads):
                    at = s * chunk_heads + h
                    kv_send[place, at : at + 1, :] = value[
                        place * steps + s : place * steps + s + 1,
                        h * HEAD_SIZE : (h + 1) * HEAD_SIZE,
                    ]
        send_rows("kv", kv_send, lambda i: kv_recv.at[i], kv_send_sem, kv_recv_sem)
        kv_recv[t] = kv_send[t]

    per_group = query_columns // HEAD_SIZE // 2 // chunk_heads

    def finish_query(c):
        value = total(c + 1)
        half, inside = c // per_group, c % per_group
        for h in range(chunk_heads):
            stage[half, :, inside * chunk_heads + h, :] = value[
                :, h * HEAD_SIZE : (h + 1) * HEAD_SIZE
            ]
        if inside == per_group - 1:
            query_send[half] = (
                stage[half].astype(jnp.bfloat16).reshape(tp_count, steps, -1, HEAD_SIZE)
            )
            send_rows(
                half,
                query_send.at[half],
                lambda i: query_recv.at[half, i],
                query_send_sem.at[half],
                query_recv_sem.at[half],
            )
            query_recv[half, t] = query_send[half, t]

    def adapted(c, value):
        return value + jnp.dot(
            low_masked[...],
            up[:, c * CHUNK : (c + 1) * CHUNK],
            preferred_element_type=jnp.float32,
        )

    heads_of = per_group * chunk_heads

    def attend_half(half):
        if half == 0:
            load_cache.wait()
            for copy in arrivals["kv"]:
                copy.wait_recv()
        for copy in arrivals[half]:
            copy.wait_recv()
        length = cache_length[0]
        scale = HEAD_SIZE**-0.5
        valid = lax.broadcasted_iota(jnp.int32, (steps * heads_of, positions), 1) < length
        extra = steps * chunk_heads
        column = lax.broadcasted_iota(jnp.int32, (steps * heads_of, extra), 1)
        step_of = lax.broadcasted_iota(jnp.int32, (steps * heads_of, extra), 0) // heads_of
        causal = column // chunk_heads <= step_of
        for tt in range(tp_count):
            g = 2 * tt + half
            query = query_recv[half, tt].reshape(steps * heads_of, HEAD_SIZE)
            keys = cache[:, g * HEAD_SIZE : (g + 1) * HEAD_SIZE]
            values = cache[:, half_width + g * HEAD_SIZE : half_width + (g + 1) * HEAD_SIZE]
            holder, inner = g // chunk_heads, g % chunk_heads
            new_keys = kv_recv[holder].astype(jnp.bfloat16)
            new_values = kv_recv[tp_count // 2 + holder].astype(jnp.bfloat16).astype(jnp.float32)
            contract = (((1,), (1,)), ((), ()))
            older = (
                lax.dot_general(query, keys, contract, preferred_element_type=jnp.float32) * scale
            )
            newer = (
                lax.dot_general(query, new_keys, contract, preferred_element_type=jnp.float32)
                * scale
            )
            older = jnp.where(valid, older, -jnp.inf)
            newer = jnp.where(
                causal & (lax.rem(column, chunk_heads) == inner), newer, -jnp.inf
            )
            top = jnp.maximum(
                jnp.max(older, axis=1, keepdims=True), jnp.max(newer, axis=1, keepdims=True)
            )
            older = jnp.exp(older - top)
            newer = jnp.exp(newer - top)
            whole = jnp.sum(older, axis=1, keepdims=True) + jnp.sum(newer, axis=1, keepdims=True)
            older = (older / whole).astype(jnp.bfloat16)
            newer = (newer / whole).astype(jnp.bfloat16).astype(jnp.float32)
            mixed = jnp.dot(older, values, preferred_element_type=jnp.float32)
            for s in range(steps):
                at = s * chunk_heads + inner
                mixed = mixed + newer[:, at : at + 1] * new_values[at : at + 1, :]
            mix[g] = mixed
            for m in range(heads_of):
                at = (g * heads_of + m) * HEAD_SIZE
                out[:, at : at + HEAD_SIZE] = mix[g, pl.ds(m, steps, stride=heads_of), :].astype(
                    jnp.bfloat16
                )

    send_parts(0, multiply(0))
    for c in range(DEFER):
        held[c] = multiply(c + 1)
    for d, (_, arrival) in enumerate(low_copies):
        if d == 0:
            pl.when(r != t)(arrival.wait_recv)
        else:
            arrival.wait_recv()
    low_total = low_recv[0]
    for i in range(1, rep_count):
        low_total = low_total + low_recv[i]
    low_masked[...] = jnp.where(matched, low_total, 0.0).astype(jnp.bfloat16)[:, 0:rank]
    load_up.wait()
    for c in range(DEFER):
        send_parts(c + 1, adapted(c, held[c]))
    finish_key_value()
    for c in range(DEFER, query_chunks):
        send_parts(c + 1, adapted(c, multiply(c + 1)))
        finish_query(c - DEFER)
    attended = per_group <= query_chunks - DEFER
    if attended:
        attend_half(0)
    for c in range(query_chunks - DEFER, query_chunks):
        finish_query(c)
    if not attended:
        attend_half(0)
    attend_half(1)

    for copy in sends:
        copy.wait_send()
    for d, (copy, _) in enumerate(low_copies):
        if d == 0:
            pl.when(r != t)(copy.wait_send)
        else:
            copy.wait_send()


def fused(*operands):
    tokens, query_weight, key_value_weight, down, up, request_tenant, slots, cache, lengths = operands
    tp_count = lax.axis_size("tp")
    rep_count = lax.axis_size("rep")
    steps, rows_rep, depth = tokens.shape
    columns = query_weight.shape[1]
    chunks = columns // CHUNK + 1
    group_rows = steps * tp_count
    rows = group_rows * rep_count
    heads_of = columns // HEAD_SIZE // 2
    rank = down.shape[2]
    bf16, f32 = jnp.bfloat16, jnp.float32
    dma = pltpu.SemaphoreType.DMA
    anywhere = pl.BlockSpec(memory_space=pl.ANY)
    scalars = pl.BlockSpec(memory_space=pltpu.SMEM)
    heads = tp_count * columns // HEAD_SIZE
    result = pl.pallas_call(
        functools.partial(fused_kernel, tp_count, rep_count),
        out_shape=jax.ShapeDtypeStruct((steps, heads * HEAD_SIZE), bf16),
        in_specs=[anywhere] * 5 + [scalars] * 2 + [anywhere, scalars],
        out_specs=pl.BlockSpec(memory_space=pltpu.VMEM),
        scratch_shapes=[
            pltpu.VMEM(tokens.shape, bf16),
            pltpu.VMEM((2 * steps * rows_rep, depth // 2), f32),
            pltpu.VMEM((tp_count, 2 * steps * rows_rep, depth // 2), bf16),
            pltpu.VMEM((rows, depth), bf16),
            pltpu.VMEM((chunks, depth, CHUNK), bf16),
            pltpu.VMEM((rank, depth), bf16),
            pltpu.VMEM(up.shape[1:], bf16),
            pltpu.VMEM(cache.shape[1:], bf16),
            pltpu.VMEM((rows, HEAD_SIZE), f32),
            pltpu.VMEM((rep_count, rows, HEAD_SIZE), f32),
            pltpu.VMEM((rows, rank), bf16),
            pltpu.VMEM((DEFER, rows, CHUNK), f32),
            pltpu.VMEM((chunks, rep_count, group_rows, CHUNK), f32),
            pltpu.VMEM((chunks, rep_count, group_rows, CHUNK), f32),
            pltpu.VMEM((2, group_rows, heads_of, HEAD_SIZE), f32),
            pltpu.VMEM((2, tp_count, steps, heads_of, HEAD_SIZE), bf16),
            pltpu.VMEM((2, tp_count, steps, heads_of, HEAD_SIZE), bf16),
            pltpu.VMEM((tp_count, steps * CHUNK // HEAD_SIZE, HEAD_SIZE), f32),
            pltpu.VMEM((tp_count, steps * CHUNK // HEAD_SIZE, HEAD_SIZE), f32),
            pltpu.VMEM((2 * tp_count, steps * heads_of, HEAD_SIZE), f32),
            dma((chunks,)),
            dma((4,)),
            dma((tp_count,)),
            dma((tp_count,)),
            dma((tp_count,)),
            dma((rep_count,)),
            dma((chunks, rep_count)),
            dma((chunks, rep_count)),
            dma((2, tp_count)),
            dma((2, tp_count)),
            dma((tp_count,)),
            dma((tp_count,)),
        ],
        compiler_params=pltpu.CompilerParams(
            collective_id=0, has_side_effects=True, vmem_limit_bytes=60 * 1024 * 1024
        ),
    )(
        tokens,
        query_weight,
        key_value_weight,
        jnp.transpose(down, (0, 2, 1)),
        up,
        jnp.transpose(request_tenant),
        slots,
        cache,
        lengths,
    )
    return result.reshape(steps, 1, heads * HEAD_SIZE)


def fits(tokens, query_weight, key_value_weight, down, up, request_tenant, slots, cache, lengths):
    tp_count = lax.axis_size("tp")
    rep_count = lax.axis_size("rep")
    columns = query_weight.shape[1]
    return (
        tp_count == rep_count
        and tp_count % 2 == 0
        and tokens.shape[0] == 2
        and tokens.shape[0] * tp_count == 8
        and tokens.shape[1] == rep_count
        and down.shape[0] == 1
        and up.shape[0] == 1
        and cache.shape[0] == 1
        and key_value_weight.shape[1] == CHUNK
        and columns == 2 * 16 * HEAD_SIZE
        and tokens.shape[2] <= 4096
    )


def slot_lookup(request_tenant, tenant_adapter_slot):
    labels = jnp.arange(tenant_adapter_slot.shape[0], dtype=jnp.int32)
    return jnp.sum(
        jnp.where(request_tenant == labels[None, :], tenant_adapter_slot[None, :], 0), axis=1
    )


def attend(query_matrix, incoming_key_value, key_value_cache, cache_length_per_row):
    row_indices = query_matrix.shape[0]
    position_span = key_value_cache.shape[1]
    incoming_token = incoming_key_value.shape[0]
    half_width = KEY_VALUE_HEADS * HEAD_SIZE
    head_outputs = query_matrix.reshape(row_indices, KEY_VALUE_HEADS, -1, HEAD_SIZE)
    stored_keys = key_value_cache[:, :, :half_width].reshape(
        row_indices, position_span, KEY_VALUE_HEADS, HEAD_SIZE
    )
    stored_values = key_value_cache[:, :, half_width:].reshape(
        row_indices, position_span, KEY_VALUE_HEADS, HEAD_SIZE
    )
    incoming_keys = jnp.transpose(incoming_key_value[:, :, :half_width], (1, 0, 2)).reshape(
        row_indices, incoming_token, KEY_VALUE_HEADS, HEAD_SIZE
    )
    incoming_values = jnp.transpose(incoming_key_value[:, :, half_width:], (1, 0, 2)).reshape(
        row_indices, incoming_token, KEY_VALUE_HEADS, HEAD_SIZE
    )
    scale = HEAD_SIZE ** (-0.5)
    older = (
        jnp.einsum("bgmd,bjgd->bgmj", head_outputs, stored_keys, preferred_element_type=jnp.float32)
        * scale
    )
    newer = (
        jnp.einsum(
            "bgmd,bjgd->bgmj", head_outputs, incoming_keys, preferred_element_type=jnp.float32
        )
        * scale
    )
    valid = jnp.arange(position_span, dtype=jnp.int32)[None, :] < cache_length_per_row[:, None]
    older = jnp.where(valid[:, None, None, :], older, -jnp.inf)
    top = jnp.maximum(jnp.max(older, axis=-1), jnp.max(newer, axis=-1))[..., None]
    older_exp = jnp.exp(older - top)
    newer_exp = jnp.exp(newer - top)
    total = jnp.sum(older_exp, axis=-1, keepdims=True) + jnp.sum(newer_exp, axis=-1, keepdims=True)
    older_prob = (older_exp / total).astype(jnp.bfloat16)
    newer_prob = (newer_exp / total).astype(jnp.bfloat16)
    mixed = jnp.einsum(
        "bgmj,bjgd->bgmd", older_prob, stored_values, preferred_element_type=jnp.float32
    )
    mixed = mixed + jnp.einsum(
        "bgmj,bjgd->bgmd", newer_prob, incoming_values, preferred_element_type=jnp.float32
    )
    return mixed.astype(jnp.bfloat16).reshape(row_indices, -1)


def shards(
    tokens,
    query_weight,
    key_value_weight,
    adapter_down_weight,
    adapter_up_weight,
    request_tenant,
    tenant_adapter_slot,
    key_value_cache,
    cache_length_per_row,
):
    operands = (
        tokens,
        query_weight,
        key_value_weight,
        adapter_down_weight,
        adapter_up_weight,
        request_tenant,
        tenant_adapter_slot,
        key_value_cache,
        cache_length_per_row,
    )
    if fits(*operands):
        return fused(*operands)
    tp_count = lax.axis_size("tp")
    rep_count = lax.axis_size("rep")
    rep_place = lax.axis_index("rep")
    rows_all = request_tenant.shape[0]
    request_slots = adapter_down_weight.shape[0]
    replicated_slots = adapter_up_weight.shape[0]
    adapter_rank_size = adapter_down_weight.shape[2]
    query_columns = query_weight.shape[1]
    kv_cols = key_value_weight.shape[1]
    local_rows = rows_all // (tp_count * rep_count)
    slot_row = slot_lookup(request_tenant, tenant_adapter_slot)
    flattened_down_weight = jnp.transpose(adapter_down_weight, (1, 0, 2)).reshape(
        adapter_down_weight.shape[1], request_slots * adapter_rank_size
    )
    flattened_up_weight = adapter_up_weight.reshape(
        replicated_slots * adapter_rank_size, query_columns
    )
    rep_labels = rep_place * replicated_slots + jnp.arange(replicated_slots, dtype=jnp.int32)
    rep_match = slot_row[:, None] == rep_labels[None, :]
    steps = tokens.shape[0]
    count = tokens.shape[0]
    piece = lax.all_gather(tokens, "tp", axis=1, tiled=True)
    flat = piece.reshape(-1, piece.shape[2])
    joined = jnp.concatenate(
        [
            jnp.dot(flat, query_weight, preferred_element_type=jnp.float32),
            jnp.dot(flat, key_value_weight, preferred_element_type=jnp.float32),
            jnp.dot(flat, flattened_down_weight, preferred_element_type=jnp.float32),
        ],
        axis=1,
    )
    terms = joined.reshape(piece.shape[0], piece.shape[1], -1)
    q_part = terms[:, :, :query_columns]
    kv_part = terms[:, :, query_columns : query_columns + kv_cols]
    low_part = terms[:, :, query_columns + kv_cols :]
    low_sum = lax.psum(low_part, "rep")
    low_all = lax.all_gather(low_sum.astype(jnp.bfloat16), "tp", axis=2, tiled=True)
    low_rep = lax.dynamic_slice_in_dim(
        low_all,
        rep_place * replicated_slots * adapter_rank_size,
        replicated_slots * adapter_rank_size,
        2,
    )
    low_rep = low_rep.reshape(count, rows_all, replicated_slots, adapter_rank_size)
    masked = jnp.where(rep_match[None, :, :, None], low_rep, jnp.zeros((), jnp.bfloat16))
    delta = jnp.dot(
        masked.reshape(count * rows_all, replicated_slots * adapter_rank_size),
        flattened_up_weight,
        preferred_element_type=jnp.float32,
    )
    q_part = (q_part + delta.reshape(count, rows_all, query_columns)).reshape(
        count, tp_count, rep_count * local_rows, query_columns
    )
    kv_part = kv_part.reshape(count, tp_count, rep_count * local_rows, kv_cols)
    q_sum = lax.psum_scatter(q_part, "rep", scatter_dimension=2, tiled=True)
    kv_sum = lax.psum_scatter(kv_part, "rep", scatter_dimension=2, tiled=True)
    query_vector = lax.all_to_all(
        q_sum.astype(jnp.bfloat16), "tp", split_axis=1, concat_axis=3, tiled=True
    )
    key_value_rows = lax.all_to_all(
        kv_sum.astype(jnp.bfloat16), "tp", split_axis=1, concat_axis=3, tiled=True
    )
    query_vector, key_value_rows = (
        query_vector.reshape(count, local_rows, -1),
        key_value_rows.reshape(count, local_rows, -1),
    )
    results = []
    for step in range(steps):
        results.append(
            attend(
                query_vector[step],
                key_value_rows[: step + 1],
                key_value_cache,
                cache_length_per_row,
            )
        )
    return jnp.stack(results)


def solution(mesh):
    placed = (
        P(None, ("groups", "tp"), "rep"),
        P("rep", "tp"),
        P("rep", "tp"),
        P(("groups", "tp"), "rep", None),
        P(("groups", "rep"), None, "tp"),
        P("groups", None),
        P(),
        P(("groups", "tp", "rep"), None, None),
        P(("groups", "tp", "rep")),
    )
    return jax.shard_map(
        shards,
        mesh=mesh,
        in_specs=placed,
        out_specs=P(None, ("groups", "tp", "rep"), None),
        check_vma=False,
    )
```

```python
import functools

import jax
import jax.numpy as jnp
from jax import lax
from jax.experimental import pallas as pl
from jax.experimental.pallas import tpu as pltpu
from jax.sharding import PartitionSpec as P

KEY_VALUE_HEADS = 8
HEAD_SIZE = 128
CHUNK = 512
DEFER = 2
LAG = 8
BEFORE = 2
AHEAD = 9
MESH = pl.DeviceIdType.MESH


def peer(tp, rep):
    return {"tp": tp, "rep": rep}


def remote(src, dst, send_sem, recv_sem, tp, rep):
    return pltpu.make_async_remote_copy(
        src_ref=src,
        dst_ref=dst,
        send_sem=send_sem,
        recv_sem=recv_sem,
        device_id=peer(tp, rep),
        device_id_type=MESH,
    )


def fused_kernel(
    tp_count,
    rep_count,
    tokens,
    query_weight,
    key_value_weight,
    adapter_down_weight,
    adapter_up_weight,
    request_tenant,
    tenant_adapter_slot,
    key_value_cache,
    cache_length,
    out,
    own_tokens,
    own_wide,
    gathered,
    hidden,
    weights,
    down,
    up,
    cache,
    low_send,
    low_recv,
    low_masked,
    held,
    part_send,
    part_recv,
    stage,
    query_send,
    query_recv,
    kv_send,
    kv_recv,
    mix,
    weight_sem,
    load_sem,
    gather_send_sem,
    gather_recv_sem,
    low_send_sem,
    low_recv_sem,
    part_send_sem,
    part_recv_sem,
    query_send_sem,
    query_recv_sem,
    kv_send_sem,
    kv_recv_sem,
):
    t = lax.axis_index("tp")
    r = lax.axis_index("rep")
    steps, rows_rep, depth = tokens.shape
    half_depth = depth // 2
    group_rows = steps * tp_count
    rows = group_rows * rep_count
    query_columns = query_weight.shape[1]
    query_chunks = query_columns // CHUNK
    chunk_heads = CHUNK // HEAD_SIZE
    rank = adapter_down_weight.shape[1]
    positions = key_value_cache.shape[1]
    half_width = KEY_VALUE_HEADS * HEAD_SIZE

    barrier = pltpu.get_barrier_semaphore()
    for dt in range(tp_count):
        for dr in range(rep_count):
            if dt or dr:
                pl.semaphore_signal(
                    barrier,
                    inc=1,
                    device_id=peer(lax.rem(t + dt, tp_count), lax.rem(r + dr, rep_count)),
                    device_id_type=MESH,
                )

    load_tokens = pltpu.make_async_copy(tokens, own_tokens, load_sem.at[0])
    load_down = pltpu.make_async_copy(adapter_down_weight.at[0], down, load_sem.at[1])
    load_up = pltpu.make_async_copy(adapter_up_weight.at[0], up, load_sem.at[2])
    load_cache = pltpu.make_async_copy(key_value_cache.at[0], cache, load_sem.at[3])
    load_tokens.start()
    load_down.start()
    load_weights = [
        pltpu.make_async_copy(key_value_weight, weights.at[0], weight_sem.at[0])
    ] + [
        pltpu.make_async_copy(
            query_weight.at[:, pl.ds(c * CHUNK, CHUNK)], weights.at[c + 1], weight_sem.at[c + 1]
        )
        for c in range(query_chunks)
    ]
    load_up.start()
    started = []

    def start_until(count):
        while len(started) < min(count, query_chunks + 1):
            load_weights[len(started)].start()
            started.append(True)
            if len(started) == query_chunks + 1:
                load_cache.start()

    start_until(BEFORE)

    load_tokens.wait()
    for s in range(steps):
        wide = own_tokens[s].astype(jnp.float32)
        for h in range(2):
            first = h * steps * rows_rep + s * rows_rep
            own_wide[first : first + rows_rep, :] = wide[:, h * half_depth : (h + 1) * half_depth]
    gathered[t] = own_wide[...].astype(jnp.bfloat16)
    pl.semaphore_wait(barrier, tp_count * rep_count - 1)

    sends = []
    gathers = []
    for d in range(tp_count - 1, 0, -1):
        to = lax.rem(t + d, tp_count)
        copy = remote(
            gathered.at[t], gathered.at[t], gather_send_sem.at[to], gather_recv_sem.at[t], to, r
        )
        copy.start()
        sends.append(copy)
        gathers.append(
            remote(
                gathered.at[to], gathered.at[to], gather_send_sem.at[to], gather_recv_sem.at[to], to, r
            )
        )

    start_until(AHEAD)

    row = lax.broadcasted_iota(jnp.int32, (rows, HEAD_SIZE), 0)
    request = lax.rem(row // steps, tp_count) * rep_count + row // group_rows
    tenant = jnp.zeros_like(row)
    for i in range(tp_count * rep_count):
        tenant = jnp.where(request == i, request_tenant[0, i], tenant)
    slot = jnp.zeros_like(row)
    for label in range(tenant_adapter_slot.shape[0]):
        slot = jnp.where(tenant == label, tenant_adapter_slot[label], slot)
    matched = slot == r

    picked = lax.broadcasted_iota(jnp.int32, (rows, 2 * rows), 0)
    place = lax.broadcasted_iota(jnp.int32, (rows, 2 * rows), 1)
    source = (
        lax.rem(picked // steps, tp_count) * (2 * steps * rows_rep)
        + lax.rem(picked, steps) * rows_rep
        + picked // group_rows
    )

    for copy in gathers:
        copy.wait_recv()
    everything = gathered[...].reshape(2 * rows, half_depth)
    for h in range(2):
        order = jnp.where(place == source + h * steps * rows_rep, 1.0, 0.0).astype(jnp.bfloat16)
        hidden[:, h * half_depth : (h + 1) * half_depth] = jnp.dot(
            order, everything, preferred_element_type=jnp.float32
        ).astype(jnp.bfloat16)

    load_down.wait()
    low_send[...] = jnp.zeros_like(low_send)
    low_send[:, 0:rank] = lax.dot_general(
        hidden[...], down[...], (((1,), (1,)), ((), ())), preferred_element_type=jnp.float32
    )
    low_copies = []
    for d in range(tp_count):
        to = lax.rem(t + d, tp_count)
        source_rep = lax.rem(t + d, rep_count)
        copy = remote(low_send, low_recv.at[r], low_send_sem.at[d], low_recv_sem.at[r], to, t)
        arrival = remote(
            low_send,
            low_recv.at[source_rep],
            low_send_sem.at[d],
            low_recv_sem.at[source_rep],
            to,
            t,
        )
        low_copies.append((copy, arrival))
        if d == 0:
            pl.when(r != t)(copy.start)
        else:
            copy.start()

    @pl.when(r == t)
    def _():
        low_recv[r] = low_send[...]

    def multiply(c):
        load_weights[c].wait()
        start_until(c + 1 + AHEAD)
        return jnp.dot(hidden[...], weights[c], preferred_element_type=jnp.float32)

    def send_parts(c, value):
        part_send[c] = value.reshape(rep_count, group_rows, CHUNK)
        for d in range(1, rep_count):
            to = lax.rem(r + d, rep_count)
            copy = remote(
                part_send.at[c, to],
                part_recv.at[c, r],
                part_send_sem.at[c, to],
                part_recv_sem.at[c, r],
                t,
                to,
            )
            copy.start()
            sends.append(copy)

    def total(c):
        value = part_send[c, r]
        for d in range(1, rep_count):
            place = lax.rem(r + d, rep_count)
            remote(
                part_send.at[c, place],
                part_recv.at[c, place],
                part_send_sem.at[c, place],
                part_recv_sem.at[c, place],
                t,
                place,
            ).wait_recv()
            value = value + part_recv[c, place]
        return value

    arrivals = {}

    def send_rows(name, source_buffer, place_of, send_sem, recv_sem):
        arrivals[name] = []
        for d in range(tp_count - 1, 0, -1):
            to = lax.rem(t + d, tp_count)
            copy = remote(
                source_buffer.at[to], place_of(t), send_sem.at[to], recv_sem.at[t], to, r
            )
            copy.start()
            sends.append(copy)
            arrivals[name].append(
                remote(source_buffer.at[to], place_of(to), send_sem.at[to], recv_sem.at[to], to, r)
            )

    def finish_key_value():
        value = total(0)
        for place in range(tp_count):
            for s in range(steps):
                for h in range(chunk_heads):
                    at = s * chunk_heads + h
                    kv_send[place, at : at + 1, :] = value[
                        place * steps + s : place * steps + s + 1,
                        h * HEAD_SIZE : (h + 1) * HEAD_SIZE,
                    ]
        send_rows("kv", kv_send, lambda i: kv_recv.at[i], kv_send_sem, kv_recv_sem)
        kv_recv[t] = kv_send[t]

    per_group = query_columns // HEAD_SIZE // 2 // chunk_heads

    def finish_query(c):
        value = total(c + 1)
        half, inside = c // per_group, c % per_group
        for h in range(chunk_heads):
            stage[half, :, inside * chunk_heads + h, :] = value[
                :, h * HEAD_SIZE : (h + 1) * HEAD_SIZE
            ]
        if inside == per_group - 1:
            query_send[half] = (
                stage[half].astype(jnp.bfloat16).reshape(tp_count, steps, -1, HEAD_SIZE)
            )
            send_rows(
                half,
                query_send.at[half],
                lambda i: query_recv.at[half, i],
                query_send_sem.at[half],
                query_recv_sem.at[half],
            )
            query_recv[half, t] = query_send[half, t]

    def adapted(c, value):
        return value + jnp.dot(
            low_masked[...],
            up[:, c * CHUNK : (c + 1) * CHUNK],
            preferred_element_type=jnp.float32,
        )

    heads_of = per_group * chunk_heads

    def attend_half(half):
        if half == 0:
            load_cache.wait()
            for copy in arrivals["kv"]:
                copy.wait_recv()
        for copy in arrivals[half]:
            copy.wait_recv()
        length = cache_length[0]
        scale = HEAD_SIZE**-0.5
        valid = lax.broadcasted_iota(jnp.int32, (steps * heads_of, positions), 1) < length
        extra = steps * chunk_heads
        column = lax.broadcasted_iota(jnp.int32, (steps * heads_of, extra), 1)
        step_of = lax.broadcasted_iota(jnp.int32, (steps * heads_of, extra), 0) // heads_of
        causal = column // chunk_heads <= step_of
        for tt in range(tp_count):
            g = 2 * tt + half
            query = query_recv[half, tt].reshape(steps * heads_of, HEAD_SIZE)
            keys = cache[:, g * HEAD_SIZE : (g + 1) * HEAD_SIZE]
            values = cache[:, half_width + g * HEAD_SIZE : half_width + (g + 1) * HEAD_SIZE]
            holder, inner = g // chunk_heads, g % chunk_heads
            new_keys = kv_recv[holder].astype(jnp.bfloat16)
            new_values = kv_recv[tp_count // 2 + holder].astype(jnp.bfloat16).astype(jnp.float32)
            contract = (((1,), (1,)), ((), ()))
            older = (
                lax.dot_general(query, keys, contract, preferred_element_type=jnp.float32) * scale
            )
            newer = (
                lax.dot_general(query, new_keys, contract, preferred_element_type=jnp.float32)
                * scale
            )
            older = jnp.where(valid, older, -jnp.inf)
            newer = jnp.where(
                causal & (lax.rem(column, chunk_heads) == inner), newer, -jnp.inf
            )
            top = jnp.maximum(
                jnp.max(older, axis=1, keepdims=True), jnp.max(newer, axis=1, keepdims=True)
            )
            older = jnp.exp(older - top)
            newer = jnp.exp(newer - top)
            whole = jnp.sum(older, axis=1, keepdims=True) + jnp.sum(newer, axis=1, keepdims=True)
            older = (older / whole).astype(jnp.bfloat16)
            newer = (newer / whole).astype(jnp.bfloat16).astype(jnp.float32)
            mixed = jnp.dot(older, values, preferred_element_type=jnp.float32)
            for s in range(steps):
                at = s * chunk_heads + inner
                mixed = mixed + newer[:, at : at + 1] * new_values[at : at + 1, :]
            mix[g] = mixed
            for m in range(heads_of):
                at = (g * heads_of + m) * HEAD_SIZE
                out[:, at : at + HEAD_SIZE] = mix[g, pl.ds(m, steps, stride=heads_of), :].astype(
                    jnp.bfloat16
                )

    send_parts(0, multiply(0))
    for c in range(DEFER):
        held[c] = multiply(c + 1)
    for d, (_, arrival) in enumerate(low_copies):
        if d == 0:
            pl.when(r != t)(arrival.wait_recv)
        else:
            arrival.wait_recv()
    low_total = low_recv[0]
    for i in range(1, rep_count):
        low_total = low_total + low_recv[i]
    low_masked[...] = jnp.where(matched, low_total, 0.0).astype(jnp.bfloat16)[:, 0:rank]
    load_up.wait()
    for c in range(DEFER):
        send_parts(c + 1, adapted(c, held[c]))
    finished = 0
    for c in range(DEFER, query_chunks):
        send_parts(c + 1, adapted(c, multiply(c + 1)))
        if c >= LAG:
            if c == LAG:
                finish_key_value()
            finish_query(finished)
            finished += 1
    if finished == 0:
        finish_key_value()
    while finished < query_chunks - 1:
        finish_query(finished)
        finished += 1
    attend_half(0)
    finish_query(finished)
    attend_half(1)

    for copy in sends:
        copy.wait_send()
    for d, (copy, _) in enumerate(low_copies):
        if d == 0:
            pl.when(r != t)(copy.wait_send)
        else:
            copy.wait_send()


def fused(*operands):
    tokens, query_weight, key_value_weight, down, up, request_tenant, slots, cache, lengths = operands
    tp_count = lax.axis_size("tp")
    rep_count = lax.axis_size("rep")
    steps, rows_rep, depth = tokens.shape
    columns = query_weight.shape[1]
    chunks = columns // CHUNK + 1
    group_rows = steps * tp_count
    rows = group_rows * rep_count
    heads_of = columns // HEAD_SIZE // 2
    rank = down.shape[2]
    bf16, f32 = jnp.bfloat16, jnp.float32
    dma = pltpu.SemaphoreType.DMA
    anywhere = pl.BlockSpec(memory_space=pl.ANY)
    scalars = pl.BlockSpec(memory_space=pltpu.SMEM)
    heads = tp_count * columns // HEAD_SIZE
    result = pl.pallas_call(
        functools.partial(fused_kernel, tp_count, rep_count),
        out_shape=jax.ShapeDtypeStruct((steps, heads * HEAD_SIZE), bf16),
        in_specs=[anywhere] * 5 + [scalars] * 2 + [anywhere, scalars],
        out_specs=pl.BlockSpec(memory_space=pltpu.VMEM),
        scratch_shapes=[
            pltpu.VMEM(tokens.shape, bf16),
            pltpu.VMEM((2 * steps * rows_rep, depth // 2), f32),
            pltpu.VMEM((tp_count, 2 * steps * rows_rep, depth // 2), bf16),
            pltpu.VMEM((rows, depth), bf16),
            pltpu.VMEM((chunks, depth, CHUNK), bf16),
            pltpu.VMEM((rank, depth), bf16),
            pltpu.VMEM(up.shape[1:], bf16),
            pltpu.VMEM(cache.shape[1:], bf16),
            pltpu.VMEM((rows, HEAD_SIZE), f32),
            pltpu.VMEM((rep_count, rows, HEAD_SIZE), f32),
            pltpu.VMEM((rows, rank), bf16),
            pltpu.VMEM((DEFER, rows, CHUNK), f32),
            pltpu.VMEM((chunks, rep_count, group_rows, CHUNK), f32),
            pltpu.VMEM((chunks, rep_count, group_rows, CHUNK), f32),
            pltpu.VMEM((2, group_rows, heads_of, HEAD_SIZE), f32),
            pltpu.VMEM((2, tp_count, steps, heads_of, HEAD_SIZE), bf16),
            pltpu.VMEM((2, tp_count, steps, heads_of, HEAD_SIZE), bf16),
            pltpu.VMEM((tp_count, steps * CHUNK // HEAD_SIZE, HEAD_SIZE), f32),
            pltpu.VMEM((tp_count, steps * CHUNK // HEAD_SIZE, HEAD_SIZE), f32),
            pltpu.VMEM((2 * tp_count, steps * heads_of, HEAD_SIZE), f32),
            dma((chunks,)),
            dma((4,)),
            dma((tp_count,)),
            dma((tp_count,)),
            dma((tp_count,)),
            dma((rep_count,)),
            dma((chunks, rep_count)),
            dma((chunks, rep_count)),
            dma((2, tp_count)),
            dma((2, tp_count)),
            dma((tp_count,)),
            dma((tp_count,)),
        ],
        compiler_params=pltpu.CompilerParams(
            collective_id=0, has_side_effects=True, vmem_limit_bytes=60 * 1024 * 1024
        ),
    )(
        tokens,
        query_weight,
        key_value_weight,
        jnp.transpose(down, (0, 2, 1)),
        up,
        jnp.transpose(request_tenant),
        slots,
        cache,
        lengths,
    )
    return result.reshape(steps, 1, heads * HEAD_SIZE)


def fits(tokens, query_weight, key_value_weight, down, up, request_tenant, slots, cache, lengths):
    tp_count = lax.axis_size("tp")
    rep_count = lax.axis_size("rep")
    columns = query_weight.shape[1]
    return (
        tp_count == rep_count
        and tp_count % 2 == 0
        and tokens.shape[0] == 2
        and tokens.shape[0] * tp_count == 8
        and tokens.shape[1] == rep_count
        and down.shape[0] == 1
        and up.shape[0] == 1
        and cache.shape[0] == 1
        and key_value_weight.shape[1] == CHUNK
        and columns == 2 * 16 * HEAD_SIZE
        and tokens.shape[2] <= 4096
    )


def slot_lookup(request_tenant, tenant_adapter_slot):
    labels = jnp.arange(tenant_adapter_slot.shape[0], dtype=jnp.int32)
    return jnp.sum(
        jnp.where(request_tenant == labels[None, :], tenant_adapter_slot[None, :], 0), axis=1
    )


def attend(query_matrix, incoming_key_value, key_value_cache, cache_length_per_row):
    row_indices = query_matrix.shape[0]
    position_span = key_value_cache.shape[1]
    incoming_token = incoming_key_value.shape[0]
    half_width = KEY_VALUE_HEADS * HEAD_SIZE
    head_outputs = query_matrix.reshape(row_indices, KEY_VALUE_HEADS, -1, HEAD_SIZE)
    stored_keys = key_value_cache[:, :, :half_width].reshape(
        row_indices, position_span, KEY_VALUE_HEADS, HEAD_SIZE
    )
    stored_values = key_value_cache[:, :, half_width:].reshape(
        row_indices, position_span, KEY_VALUE_HEADS, HEAD_SIZE
    )
    incoming_keys = jnp.transpose(incoming_key_value[:, :, :half_width], (1, 0, 2)).reshape(
        row_indices, incoming_token, KEY_VALUE_HEADS, HEAD_SIZE
    )
    incoming_values = jnp.transpose(incoming_key_value[:, :, half_width:], (1, 0, 2)).reshape(
        row_indices, incoming_token, KEY_VALUE_HEADS, HEAD_SIZE
    )
    scale = HEAD_SIZE ** (-0.5)
    older = (
        jnp.einsum("bgmd,bjgd->bgmj", head_outputs, stored_keys, preferred_element_type=jnp.float32)
        * scale
    )
    newer = (
        jnp.einsum(
            "bgmd,bjgd->bgmj", head_outputs, incoming_keys, preferred_element_type=jnp.float32
        )
        * scale
    )
    valid = jnp.arange(position_span, dtype=jnp.int32)[None, :] < cache_length_per_row[:, None]
    older = jnp.where(valid[:, None, None, :], older, -jnp.inf)
    top = jnp.maximum(jnp.max(older, axis=-1), jnp.max(newer, axis=-1))[..., None]
    older_exp = jnp.exp(older - top)
    newer_exp = jnp.exp(newer - top)
    total = jnp.sum(older_exp, axis=-1, keepdims=True) + jnp.sum(newer_exp, axis=-1, keepdims=True)
    older_prob = (older_exp / total).astype(jnp.bfloat16)
    newer_prob = (newer_exp / total).astype(jnp.bfloat16)
    mixed = jnp.einsum(
        "bgmj,bjgd->bgmd", older_prob, stored_values, preferred_element_type=jnp.float32
    )
    mixed = mixed + jnp.einsum(
        "bgmj,bjgd->bgmd", newer_prob, incoming_values, preferred_element_type=jnp.float32
    )
    return mixed.astype(jnp.bfloat16).reshape(row_indices, -1)


def shards(
    tokens,
    query_weight,
    key_value_weight,
    adapter_down_weight,
    adapter_up_weight,
    request_tenant,
    tenant_adapter_slot,
    key_value_cache,
    cache_length_per_row,
):
    operands = (
        tokens,
        query_weight,
        key_value_weight,
        adapter_down_weight,
        adapter_up_weight,
        request_tenant,
        tenant_adapter_slot,
        key_value_cache,
        cache_length_per_row,
    )
    if fits(*operands):
        return fused(*operands)
    tp_count = lax.axis_size("tp")
    rep_count = lax.axis_size("rep")
    rep_place = lax.axis_index("rep")
    rows_all = request_tenant.shape[0]
    request_slots = adapter_down_weight.shape[0]
    replicated_slots = adapter_up_weight.shape[0]
    adapter_rank_size = adapter_down_weight.shape[2]
    query_columns = query_weight.shape[1]
    kv_cols = key_value_weight.shape[1]
    local_rows = rows_all // (tp_count * rep_count)
    slot_row = slot_lookup(request_tenant, tenant_adapter_slot)
    flattened_down_weight = jnp.transpose(adapter_down_weight, (1, 0, 2)).reshape(
        adapter_down_weight.shape[1], request_slots * adapter_rank_size
    )
    flattened_up_weight = adapter_up_weight.reshape(
        replicated_slots * adapter_rank_size, query_columns
    )
    rep_labels = rep_place * replicated_slots + jnp.arange(replicated_slots, dtype=jnp.int32)
    rep_match = slot_row[:, None] == rep_labels[None, :]
    steps = tokens.shape[0]
    count = tokens.shape[0]
    piece = lax.all_gather(tokens, "tp", axis=1, tiled=True)
    flat = piece.reshape(-1, piece.shape[2])
    joined = jnp.concatenate(
        [
            jnp.dot(flat, query_weight, preferred_element_type=jnp.float32),
            jnp.dot(flat, key_value_weight, preferred_element_type=jnp.float32),
            jnp.dot(flat, flattened_down_weight, preferred_element_type=jnp.float32),
        ],
        axis=1,
    )
    terms = joined.reshape(piece.shape[0], piece.shape[1], -1)
    q_part = terms[:, :, :query_columns]
    kv_part = terms[:, :, query_columns : query_columns + kv_cols]
    low_part = terms[:, :, query_columns + kv_cols :]
    low_sum = lax.psum(low_part, "rep")
    low_all = lax.all_gather(low_sum.astype(jnp.bfloat16), "tp", axis=2, tiled=True)
    low_rep = lax.dynamic_slice_in_dim(
        low_all,
        rep_place * replicated_slots * adapter_rank_size,
        replicated_slots * adapter_rank_size,
        2,
    )
    low_rep = low_rep.reshape(count, rows_all, replicated_slots, adapter_rank_size)
    masked = jnp.where(rep_match[None, :, :, None], low_rep, jnp.zeros((), jnp.bfloat16))
    delta = jnp.dot(
        masked.reshape(count * rows_all, replicated_slots * adapter_rank_size),
        flattened_up_weight,
        preferred_element_type=jnp.float32,
    )
    q_part = (q_part + delta.reshape(count, rows_all, query_columns)).reshape(
        count, tp_count, rep_count * local_rows, query_columns
    )
    kv_part = kv_part.reshape(count, tp_count, rep_count * local_rows, kv_cols)
    q_sum = lax.psum_scatter(q_part, "rep", scatter_dimension=2, tiled=True)
    kv_sum = lax.psum_scatter(kv_part, "rep", scatter_dimension=2, tiled=True)
    query_vector = lax.all_to_all(
        q_sum.astype(jnp.bfloat16), "tp", split_axis=1, concat_axis=3, tiled=True
    )
    key_value_rows = lax.all_to_all(
        kv_sum.astype(jnp.bfloat16), "tp", split_axis=1, concat_axis=3, tiled=True
    )
    query_vector, key_value_rows = (
        query_vector.reshape(count, local_rows, -1),
        key_value_rows.reshape(count, local_rows, -1),
    )
    results = []
    for step in range(steps):
        results.append(
            attend(
                query_vector[step],
                key_value_rows[: step + 1],
                key_value_cache,
                cache_length_per_row,
            )
        )
    return jnp.stack(results)


def solution(mesh):
    placed = (
        P(None, ("groups", "tp"), "rep"),
        P("rep", "tp"),
        P("rep", "tp"),
        P(("groups", "tp"), "rep", None),
        P(("groups", "rep"), None, "tp"),
        P("groups", None),
        P(),
        P(("groups", "tp", "rep"), None, None),
        P(("groups", "tp", "rep")),
    )
    return jax.shard_map(
        shards,
        mesh=mesh,
        in_specs=placed,
        out_specs=P(None, ("groups", "tp", "rep"), None),
        check_vma=False,
    )
```
